32 devices in a mesh: section: 2 (over y), dp: 4 (over x, core), tensor: 4 (over z).
Axes of the slice: x: 2, y: 2, z: 4, core: 2. Of those that a mesh axis runs over, the one named last changes fastest.
Arguments:
- inputs: bfloat16 [8, 1024, 1024], P('dp', 'tensor'), may hold values from -6 to 6
- segment_ids: int32 [8, 1024], P('dp'), may hold values from 0 to 3, as said below
- valid_frames: int32 [8, 1024], P('dp'), may hold values from 0 to 1, as said below
- segment_codes: int32 [8, 4], P('dp'), may hold values from 0 to 7
- norm_table: float32 [2, 8, 4, 1024], P('section'), may hold values from -1.5 to 1.5
- entry_weight: bfloat16 [2, 1024, 3, 1024], P('section', 'dp', None, 'tensor'), may hold values from -0.1875 to 0.1875
- mixing_weight: bfloat16 [2, 1024, 1024], P('section', 'tensor', 'dp'), may hold values from -3 to 3
- expand_weight: bfloat16 [2, 1024, 4096], P('section', 'dp', 'tensor'), may hold values from -0.1875 to 0.1875
- contract_weight: bfloat16 [2, 4096, 1024], P('section', 'tensor', 'dp'), may hold values from -0.09375 to 0.09375
- cotangent: bfloat16 [2, 8, 1024, 1024], P('section', 'dp', 'tensor'), may hold values from -6 to 6
Outputs:
- layer_outputs: bfloat16 [2, 8, 1024, 1024], P('section', 'dp', 'tensor')
- input_grads: float32 [2, 8, 1024, 1024], P('section', 'dp', 'tensor')
- entry_grad: float32 [2, 1024, 3, 1024], P('section', 'dp', None, 'tensor')
- mixing_grad: float32 [2, 1024, 1024], P('section', 'tensor', 'dp')
- expand_grad: float32 [2, 1024, 4096], P('section', 'dp', 'tensor')
- contract_grad: float32 [2, 4096, 1024], P('section', 'tensor', 'dp')
- table_grad: float32 [2, 8, 4, 1024], P('section')
The draws below stay inside these ranges and needn't reach their ends.
Inputs may be any that keep to these rules, and one draw needn't show every extreme that they name: `segment_ids`: Non-decreasing along each row from 0; a row has 4 segments or a single one, and of the 2 rows of each index of dp exactly one has a single segment. `valid_frames`: in each row ones, then at most 64 zeros.
All inputs are finite; a program needn't handle non-finite values.
Results may differ from the reference program's by a relative error of at most 0.02.
Values may be sent and summed in bfloat16 or wider, within the bound.
No kernel may reach another device: no remote copies, remote signals or barrier semaphores. Data moves between devices by JAX's collectives and lax.ppermute only.
A program may use at most 128 MiB of HBM per device.

```python
import math
import jax
import jax.numpy as jnp
from jax import lax

HEAD_DIM = 64
D = 1024
FF = 4096
CODES = 8
FRAMES = 1024
MICRO = 2
SEGS = 4
ROWS = 8


def draw_segment_ids(key, part):
    key = jax.random.fold_in(key, 11)
    row_keys = jax.random.split(key, ROWS + 1)

    def one_row(row_key):
        shuffled = jax.random.permutation(row_key, FRAMES - 1) + 1
        cut_places = shuffled[:SEGS - 1]
        boundary = jnp.zeros((FRAMES,), jnp.int32).at[cut_places].set(1)
        return jnp.cumsum(boundary).astype(jnp.int32)
    numbered = jax.vmap(one_row)(row_keys[:ROWS])
    chosen = jax.random.randint(row_keys[ROWS], (ROWS // MICRO,), 0, MICRO)
    row_numbers = jnp.arange(ROWS, dtype=jnp.int32)
    single_row = row_numbers % MICRO == jnp.repeat(chosen, MICRO)
    return jnp.where(single_row[:, None], 0, numbered).astype(jnp.int32)


def draw_valid_frames(key, part):
    key = jax.random.fold_in(key, 23)
    padding = jax.random.randint(key, (ROWS, 1), 0, FRAMES // 16 + 1)
    places = jnp.arange(FRAMES, dtype=jnp.int32)[None, :]
    return (places < FRAMES - padding).astype(jnp.int32)


def set_ends(array, own_key, low, largest):
    longest = array.shape.index(max(array.shape))
    spots = []
    for shift in (0, 1):
        where = [jax.random.randint(jax.random.fold_in(own_key, axis), (), 0, length) for axis, length in enumerate(array.shape)]
        where[longest] = (where[longest] + shift) % array.shape[longest]
        spots.append(tuple(where))
    return array.at[spots[0]].set(low).at[spots[1]].set(largest)


def block_levels(own_key, shape, cuts, smallest, high):
    loudness, own = 1.0, jax.random.fold_in(own_key, 6)
    for dim, shards_of in cuts:
        heights = jnp.exp(jax.random.uniform(jax.random.fold_in(own, dim), (shards_of,), jnp.float32, smallest / len(cuts), high / len(cuts)))
        loudness = loudness * jnp.repeat(heights, shape[dim] // shards_of).reshape([-1 if axis == dim else 1 for axis in range(len(shape))])
    return loudness


def gaussian(stream_key, shape, scale, bound, shards=(), kind=jnp.bfloat16):
    loudness = block_levels(stream_key, shape, shards, -0.22, 0.18) if shards else 1.0
    values = jax.random.normal(stream_key, shape, jnp.float32) * scale * loudness
    return jnp.minimum(jnp.maximum(values, -bound), bound).astype(kind)


def setup_inputs(seed: int = 0) -> dict:
    splits = jax.random.split(jax.random.key(seed), 11)
    inputs = gaussian(splits[0], (ROWS, FRAMES, D), 1.0, 6.0, ((0, 4), (1, 4)))
    segment_ids = draw_segment_ids(jax.random.fold_in(splits[10], 71), 0)
    valid_frames = draw_valid_frames(jax.random.fold_in(splits[10], 71), 0)
    segment_codes = set_ends(jax.random.randint(splits[3], (ROWS, SEGS), 0, CODES), jax.random.fold_in(splits[3], 1), 0, CODES - 1).astype(jnp.int32)
    norm_table = gaussian(splits[4], (2, CODES, 4, D), 0.3, 1.5, ((0, 2),), jnp.float32)
    entry_weight = gaussian(splits[5], (2, D, 3, D), D ** -0.5, 0.1875, ((0, 2), (1, 4), (3, 4)))
    mixing_weight = gaussian(splits[6], (2, D, D), (max(1, D * SEGS // FRAMES)) ** -0.5, 3.0, ((0, 2), (1, 4), (2, 4)))
    expand_weight = gaussian(splits[7], (2, D, FF), D ** -0.5, 0.1875, ((0, 2), (1, 4), (2, 4)))
    contract_weight = gaussian(splits[8], (2, FF, D), FF ** -0.5, 0.09375, ((0, 2), (1, 4), (2, 4)))
    cotangent = gaussian(splits[9], (2, ROWS, FRAMES, D), 1.0, 6.0, ((0, 2), (1, 4), (2, 4)))
    return {"inputs": inputs, "segment_ids": segment_ids, "valid_frames": valid_frames, "segment_codes": segment_codes, "norm_table": norm_table, "entry_weight": entry_weight, "mixing_weight": mixing_weight, "expand_weight": expand_weight, "contract_weight": contract_weight, "cotangent": cotangent}


NORM_EPS = 1e-05
MASKED = -1e+30
HIGHEST = lax.Precision.HIGHEST

@jax.custom_vjp
def low(v):
    return lax.optimization_barrier(v.astype(jnp.bfloat16)).astype(jnp.float32)

@jax.custom_vjp
def low_back(v):
    return v

def low_keep(v):
    return (low(v), None)

def low_pass(kept, grad):
    return (grad,)

def back_keep(v):
    return (v, None)

def back_low(kept, grad):
    return (low(grad),)
low.defvjp(low_keep, low_pass)
low_back.defvjp(back_keep, back_low)

def positions_table(segment_row, features):
    places = jnp.arange(segment_row.shape[0], dtype=jnp.int32)
    earlier = jnp.concatenate([segment_row[:1] - 1, segment_row[:-1]])
    starts = lax.cummax(jnp.where(segment_row != earlier, places, 0), axis=0)
    offset = (places - starts).astype(jnp.float32)
    column = jnp.arange(features, dtype=jnp.int32)
    frequency = jnp.exp(-math.log(10000.0) * (2 * (column // 2)).astype(jnp.float32) / features)
    angles = offset[:, None] * frequency[None, :]
    return jnp.where(column[None, :] % 2 == 0, jnp.sin(angles), jnp.cos(angles))

def code_weights(segment_row, code_row, code_count):
    slots = jnp.arange(code_row.shape[0], dtype=jnp.int32)
    token_code = lax.optimization_barrier(jnp.sum(jnp.where(segment_row[:, None] == slots[None, :], code_row[None, :], 0), axis=1))
    return (token_code[:, None] == jnp.arange(code_count, dtype=jnp.int32)[None, :]).astype(jnp.float32)

def allowed_keys(segment_row, valid_row, first_row, block_rows, causal_flag):
    query_place = first_row + jnp.arange(block_rows, dtype=jnp.int32)
    key_place = jnp.arange(segment_row.shape[0], dtype=jnp.int32)
    query_segment = lax.dynamic_slice_in_dim(segment_row, first_row, block_rows, 0)
    permitted = (query_segment[:, None] == segment_row[None, :]) & (valid_row[None, :] == 1)
    permitted = permitted & ((key_place[None, :] <= query_place[:, None]) | jnp.logical_not(causal_flag))
    return permitted | (key_place[None, :] == query_place[:, None])

def adaptive_norm(values_in, scale, shift):
    centred = values_in - lax.optimization_barrier(jnp.mean(values_in, axis=-1, keepdims=True))
    spread = lax.optimization_barrier(jnp.mean(centred * centred, axis=-1, keepdims=True))
    return centred * lax.rsqrt(spread + NORM_EPS) * (1.0 + scale) + shift

def attention_rows(queries, keys_all, values_all, segment_row, valid_row, causal_flag):
    frame_count = queries.shape[0]
    blocks = max(1, frame_count // 512)
    block_rows = frame_count // blocks
    query_scale = 1.0 / math.sqrt(HEAD_DIM)

    def one_block(first_row):
        query_part = lax.dynamic_slice_in_dim(queries, first_row, block_rows, 0)
        scores = low_back(jnp.einsum('qhe,khe->hqk', query_part, keys_all, precision=HIGHEST) * query_scale)
        permitted = allowed_keys(segment_row, valid_row, first_row, block_rows, causal_flag)
        scores = jnp.where(permitted[None], scores, MASKED)
        row_peak = lax.optimization_barrier(jnp.max(scores, axis=-1, keepdims=True))
        exponent = jnp.exp(scores - row_peak)
        weights = low(exponent / lax.optimization_barrier(jnp.sum(exponent, axis=-1, keepdims=True)))
        return jnp.einsum('hqk,khe->qhe', weights, values_all, precision=HIGHEST)
    starts = jnp.arange(blocks, dtype=jnp.int32) * block_rows
    mixture = lax.map(jax.checkpoint(one_block), starts)
    return mixture.reshape(frame_count, -1)

def one_layer(stream, segment_row, valid_row, coefficients, weights, causal_flag):
    entry_all, mixing_all, expand_all, contract_all = weights
    frame_count, features = stream.shape
    normed = low(adaptive_norm(stream, coefficients[:, 0], coefficients[:, 1]))
    projected = low_back(low(jnp.dot(normed, entry_all.reshape(features, -1), precision=HIGHEST)))
    projected = projected.reshape(frame_count, 3, -1, HEAD_DIM)
    mixture = attention_rows(projected[:, 0], projected[:, 1], projected[:, 2], segment_row, valid_row, causal_flag)
    mixture = low_back(low(mixture))
    middle = stream + low_back(jnp.dot(mixture, mixing_all, precision=HIGHEST))
    second = low(adaptive_norm(middle, coefficients[:, 2], coefficients[:, 3]))
    gate_pre = low_back(jnp.dot(second, expand_all, precision=HIGHEST))
    hidden = low(jax.nn.gelu(gate_pre))
    return middle + low_back(jnp.dot(hidden, contract_all, precision=HIGHEST))

def reference(inputs, segment_ids, valid_frames, segment_codes, norm_table, entry_weight, mixing_weight, expand_weight, contract_weight, cotangent):
    features = inputs.shape[2]
    code_count = norm_table.shape[1]

    def forward(stream_in, shift_in, table_all, entry_all, mixing_all, expand_all, contract_all):

        def row_pair(pieces):
            row_input, row_shift, segment_row, valid_row, code_row = pieces
            chooser = code_weights(segment_row, code_row, code_count)
            first_scales = jnp.dot(chooser, table_all[0].reshape(code_count, -1), precision=HIGHEST).reshape(-1, 4, features)
            second_scales = jnp.dot(chooser, table_all[1].reshape(code_count, -1), precision=HIGHEST).reshape(-1, 4, features)
            first_weights = (entry_all[0], mixing_all[0], expand_all[0], contract_all[0])
            second_weights = (entry_all[1], mixing_all[1], expand_all[1], contract_all[1])
            first_out = low(one_layer(row_input + positions_table(segment_row, features), segment_row, valid_row, first_scales, first_weights, True))
            second_out = one_layer(first_out + row_shift, segment_row, valid_row, second_scales, second_weights, False)
            return (first_out, second_out)
        return lax.map(jax.checkpoint(row_pair), (stream_in, shift_in, segment_ids, valid_frames, segment_codes))
    results, pullback = jax.vjp(forward, inputs.astype(jnp.float32), jnp.zeros(inputs.shape, jnp.float32), norm_table, entry_weight.astype(jnp.float32), mixing_weight.astype(jnp.float32), expand_weight.astype(jnp.float32), contract_weight.astype(jnp.float32))
    gradients = pullback((cotangent[0].astype(jnp.float32), cotangent[1].astype(jnp.float32)))
    layer_outputs = jnp.stack((results[0], results[1])).astype(jnp.bfloat16)
    input_grads = jnp.stack((gradients[0], gradients[1]))
    return (layer_outputs, input_grads, gradients[3], gradients[4], gradients[5], gradients[6], gradients[2])
```

```python
import math

import jax
import jax.numpy as jnp
from jax import lax
from jax.experimental import pallas as pl
from jax.experimental.pallas import tpu as pltpu
from jax.sharding import Mesh, PartitionSpec as P

HEAD_DIM = 64
NORM_EPS = 1e-05
MASKED = -1e30
HIGHEST = lax.Precision.HIGHEST
PAIR = 2 * HEAD_DIM
QUERY_SCALE = 1.0 / math.sqrt(HEAD_DIM)
VMEM_LIMIT = 32 * 2**20
BF16 = jnp.bfloat16
F32 = jnp.float32


def product(left, right, left_dim, right_dim):
    return lax.dot_general(left, right, (((left_dim,), (right_dim,)), ((), ())), preferred_element_type=F32)


def partner(block, axis, step=1):
    return lax.ppermute(block, axis, [(i, i ^ step) for i in range(lax.axis_size(axis))])


def gather_waves(piece):
    waves = []
    for step in range(lax.axis_size("zl")):
        part = piece if step == 0 else partner(piece, "zl", step)
        waves.append(jnp.concatenate([part, partner(part, "core")], axis=0))
    return waves


def scatter_waves(term_of):
    total = None
    for step in reversed(range(lax.axis_size("zl"))):
        term = term_of(step)
        half = term.shape[0] // 2
        mine = term[:half] + partner(term[half:].astype(BF16), "core").astype(F32)
        if step:
            mine = partner(mine.astype(BF16), "zl", step).astype(F32)
        total = mine if total is None else total + mine
    return total


def waves_of(array):
    return jnp.split(array, lax.axis_size("zl"), axis=0)


def positions_table(offset, features):
    column = jnp.arange(features, dtype=jnp.int32)
    frequency = jnp.exp(-math.log(10000.0) * (2 * (column // 2)).astype(F32) / features)
    angles = offset.astype(F32)[:, None] * frequency[None, :]
    return jnp.where(column[None, :] % 2 == 0, jnp.sin(angles), jnp.cos(angles))


def normalize(values):
    centred = values - jnp.mean(values, axis=-1, keepdims=True)
    spread = jnp.mean(centred * centred, axis=-1, keepdims=True)
    rate = lax.rsqrt(spread + NORM_EPS)
    return centred * rate, rate


def gelu_pair(x):
    slope = math.sqrt(2.0 / math.pi)
    square = x * x
    bent = jnp.tanh(slope * x * (1.0 + 0.044715 * square))
    half = 0.5 * (1.0 + bent)
    rise = half + 0.5 * x * (1.0 - bent * bent) * (slope * (1.0 + 3.0 * 0.044715 * square))
    return x * half, rise


def head_lanes(block, side):
    lanes = lax.broadcasted_iota(jnp.int32, block.shape, 1)
    return jnp.where(lanes // HEAD_DIM == side, block, jnp.zeros_like(block))


def attend_kernel(
    query_ref, key_ref, value_ref, key_info_ref, query_info_ref, mixed_ref, logsum_ref, bias_ref
):
    key_segment, key_place = key_info_ref[:, 0:1], key_info_ref[:, 1:2]
    query_segment, query_place, last = query_info_ref[0:1, :], query_info_ref[1:2, :], query_info_ref[2:3, :]
    allowed = ((key_segment == query_segment) & (key_place <= last)) | (key_place == query_place)
    bias_ref[...] = jnp.where(allowed, 0.0, MASKED)
    rows, logsums = [], []
    for pair in range(query_ref.shape[1] // PAIR):
        lanes = slice(pair * PAIR, (pair + 1) * PAIR)
        keys, values = key_ref[:, lanes], value_ref[:, lanes]
        queries = query_ref[:, lanes] * QUERY_SCALE
        for side in range(PAIR // HEAD_DIM):
            scores = product(keys, head_lanes(queries, side), 1, 1) + bias_ref[...]
            peak = jnp.max(scores, axis=0, keepdims=True)
            raised = jnp.exp(scores - peak)
            total = jnp.sum(raised, axis=0, keepdims=True)
            mixed = product(values, raised.astype(BF16), 0, 0)
            rows.append(mixed[side * HEAD_DIM : (side + 1) * HEAD_DIM] * (1.0 / total))
            logsums.append(peak + jnp.log(total))
    mixed_ref[...] = jnp.concatenate(rows, axis=0).T.astype(BF16)
    logsum_ref[...] = jnp.concatenate(logsums, axis=0)


def attend(projected, key_info, query_info):
    frames, width = projected.shape[0], projected.shape[1] // 3
    block = min(frames, 256)
    blocks, heads = frames // block, width // HEAD_DIM
    return pl.pallas_call(
        attend_kernel,
        grid=(blocks,),
        in_specs=[
            pl.BlockSpec((block, width), lambda i: (i, 0)),
            pl.BlockSpec((frames, width), lambda i: (0, 1)),
            pl.BlockSpec((frames, width), lambda i: (0, 2)),
            pl.BlockSpec(key_info.shape, lambda i: (0, 0)),
            pl.BlockSpec((query_info.shape[0], block), lambda i: (0, i)),
        ],
        out_specs=[
            pl.BlockSpec((block, width), lambda i: (i, 0)),
            pl.BlockSpec((heads, block), lambda i: (0, i)),
        ],
        out_shape=[
            jax.ShapeDtypeStruct((frames, width), BF16),
            jax.ShapeDtypeStruct((heads, frames), F32),
        ],
        scratch_shapes=[pltpu.VMEM((frames, block), F32)],
        compiler_params=pltpu.CompilerParams(vmem_limit_bytes=VMEM_LIMIT),
        cost_estimate=pl.CostEstimate(
            flops=16 * frames * frames * width,
            bytes_accessed=8 * frames * width,
            transcendentals=heads * frames * frames,
        ),
        name="attend",
    )(projected, projected, projected, key_info, query_info)


def attend_back_kernel(
    query_ref, key_ref, value_ref, key_info_ref, query_info_ref, mixed_ref, logsum_ref, grad_ref, key_sum, value_sum, bias_ref
):
    step = pl.program_id(0)
    block, width = query_ref.shape

    @pl.when(step == 0)
    def _():
        key_sum[...] = jnp.zeros_like(key_sum)
        value_sum[...] = jnp.zeros_like(value_sum)

    key_segment, key_place = key_info_ref[:, 0:1], key_info_ref[:, 1:2]
    query_segment, query_place, last = query_info_ref[0:1, :], query_info_ref[1:2, :], query_info_ref[2:3, :]
    allowed = ((key_segment == query_segment) & (key_place <= last)) | (key_place == query_place)
    bias_ref[...] = jnp.where(allowed, 0.0, MASKED)
    rows = []
    for pair in range(width // PAIR):
        lanes = slice(pair * PAIR, (pair + 1) * PAIR)
        keys, values = key_ref[:, lanes], value_ref[:, lanes]
        queries = query_ref[:, lanes] * QUERY_SCALE
        for side in range(PAIR // HEAD_DIM):
            head = pair * (PAIR // HEAD_DIM) + side
            query_part = head_lanes(queries, side)
            upstream = head_lanes(mixed_ref[:, lanes], side)
            scores = product(keys, query_part, 1, 1) + bias_ref[...]
            probs = jnp.exp(scores - logsum_ref[head : head + 1, :])
            prob_grad = product(values, upstream, 1, 1)
            inner = jnp.sum(probs * prob_grad, axis=0, keepdims=True)
            score_grad = (probs * (prob_grad - inner)).astype(BF16)
            value_sum[:, lanes] += product(probs.astype(BF16), upstream, 1, 0)
            key_sum[:, lanes] += product(score_grad, query_part, 1, 0)
            row = product(keys, score_grad, 0, 0)
            rows.append(row[side * HEAD_DIM : (side + 1) * HEAD_DIM])
    query_grad = jnp.concatenate(rows, axis=0).T * QUERY_SCALE
    grad_ref[pl.ds(pl.multiple_of(step * block, block), block), :width] = query_grad.astype(BF16)

    @pl.when(step == pl.num_programs(0) - 1)
    def _():
        grad_ref[:, width : 2 * width] = key_sum[...].astype(BF16)
        grad_ref[:, 2 * width :] = value_sum[...].astype(BF16)


def attend_back(projected, key_info, query_info, mixture_grad, logsum):
    frames, width = mixture_grad.shape
    block = min(frames, 256)
    blocks, heads = frames // block, width // HEAD_DIM
    return pl.pallas_call(
        attend_back_kernel,
        grid=(blocks,),
        in_specs=[
            pl.BlockSpec((block, width), lambda i: (i, 0)),
            pl.BlockSpec((frames, width), lambda i: (0, 1)),
            pl.BlockSpec((frames, width), lambda i: (0, 2)),
            pl.BlockSpec(key_info.shape, lambda i: (0, 0)),
            pl.BlockSpec((query_info.shape[0], block), lambda i: (0, i)),
            pl.BlockSpec((block, width), lambda i: (i, 0)),
            pl.BlockSpec((heads, block), lambda i: (0, i)),
        ],
        out_specs=pl.BlockSpec((frames, 3 * width), lambda i: (0, 0)),
        out_shape=jax.ShapeDtypeStruct((frames, 3 * width), BF16),
        scratch_shapes=[
            pltpu.VMEM((frames, width), F32),
            pltpu.VMEM((frames, width), F32),
            pltpu.VMEM((frames, block), F32),
        ],
        compiler_params=pltpu.CompilerParams(vmem_limit_bytes=VMEM_LIMIT),
        cost_estimate=pl.CostEstimate(
            flops=40 * frames * frames * width,
            bytes_accessed=14 * frames * width,
            transcendentals=heads * frames * frames,
        ),
        name="attend_back",
    )(projected, projected, projected, key_info, query_info, mixture_grad, logsum)


def after(value, earlier):
    return lax.optimization_barrier((value, earlier))[0]


def together(*values):
    return lax.optimization_barrier(values)


def layer_forward(stream, context, table, weights, causal, at_projected, at_second):
    entry_mixing, expand, contract = weights
    width = entry_mixing.shape[1] // 4
    entry, mixing = entry_mixing[:, : 3 * width], entry_mixing[:, 3 * width :]
    scale_one, shift_one, scale_two, shift_two = table
    unit_one, rate_one = normalize(stream)
    normed = gather_waves((unit_one * (1.0 + scale_one) + shift_one).astype(BF16))
    projected = jnp.concatenate([product(wave, entry, 1, 0).astype(BF16) for wave in normed], axis=0)
    side = at_projected(projected)
    mixture, logsum = attend(projected, context["key_info"], context["query_info"][causal])
    mixture, side = together(mixture, side)
    mixture_waves = waves_of(mixture)
    middle = stream + scatter_waves(lambda step: product(mixture_waves[step], mixing, 1, 1))
    middle = lax.optimization_barrier(middle)
    unit_two, rate_two = normalize(middle)
    second = gather_waves((unit_two * (1.0 + scale_two) + shift_two).astype(BF16))
    second = at_second(second)
    pairs = [gelu_pair(product(wave, expand, 1, 0)) for wave in second]
    pairs = [together(pair[0].astype(BF16), pair[1].astype(BF16)) for pair in pairs]
    hidden, rise = [pair[0] for pair in pairs], [pair[1] for pair in pairs]
    result = middle + scatter_waves(lambda step: product(hidden[step], contract, 1, 1))
    join = lambda waves: jnp.concatenate(waves, axis=0)
    saved = (unit_one, rate_one, unit_two, rate_two, join(normed), projected, mixture, logsum, join(second), join(hidden), rise)
    return result, saved, side


def norm_back(unit, rate, scale, grad, chosen):
    lifted = grad * (1.0 + scale)
    back = rate * (
        lifted
        - jnp.mean(lifted, axis=-1, keepdims=True)
        - unit * jnp.mean(lifted * unit, axis=-1, keepdims=True)
    )
    scale_sum = lax.dot_general(chosen, grad * unit, (((0,), (0,)), ((), ())), precision=HIGHEST)
    shift_sum = lax.dot_general(chosen, grad, (((0,), (0,)), ((), ())), precision=HIGHEST)
    return back, scale_sum, shift_sum


def layer_backward(saved, context, table, weights, upstream, branch, causal, at_second, at_outgoing, at_projected):
    unit_one, rate_one, unit_two, rate_two, normed, projected, mixture, logsum, second, hidden, rise = saved
    entry_mixing, expand, contract = weights
    width = entry_mixing.shape[1] // 4
    entry, mixing = entry_mixing[:, : 3 * width], entry_mixing[:, 3 * width :]
    scale_one, shift_one, scale_two, shift_two = table
    gate_grad = [
        (product(wave, contract, 1, 0) * steep.astype(F32)).astype(BF16) for wave, steep in zip(branch, rise)
    ]
    second_grad = scatter_waves(lambda step: product(gate_grad[step], expand, 1, 1))
    branch, gate_grad = jnp.concatenate(branch, axis=0), jnp.concatenate(gate_grad, axis=0)
    terms = (product(branch, hidden, 0, 0).astype(BF16), product(second, gate_grad, 0, 0).astype(BF16))
    second_grad, terms = together(second_grad, terms)
    contract_part, expand_part = reduce_weight(terms[0]), reduce_weight(terms[1])
    second_grad = at_second(second_grad)
    part, scale_two_sum, shift_two_sum = norm_back(unit_two, rate_two, scale_two, second_grad, context["chosen"])
    middle_grad = upstream + part
    outgoing = gather_waves(middle_grad.astype(BF16))
    outgoing = at_outgoing(outgoing)
    mixture_grad = jnp.concatenate([product(wave, mixing, 1, 0).astype(BF16) for wave in outgoing], axis=0)
    mixing_term = product(jnp.concatenate(outgoing, axis=0), mixture, 0, 0).astype(BF16)
    projected_grad = attend_back(
        projected, context["key_info"], context["query_info"][causal], mixture_grad, logsum
    )
    projected_grad = at_projected(projected_grad)
    term = jnp.concatenate((product(normed, projected_grad, 0, 0).astype(BF16), mixing_term), axis=1)
    projected_grad, term = together(projected_grad, term)
    entry_part = reduce_weight(term)
    projected_waves = waves_of(projected_grad)
    normed_grad = scatter_waves(lambda step: product(projected_waves[step], entry, 1, 1))
    part, scale_one_sum, shift_one_sum = norm_back(unit_one, rate_one, scale_one, normed_grad, context["chosen"])
    table_term = jnp.stack((scale_one_sum, shift_one_sum, scale_two_sum, shift_two_sum), axis=1)
    return middle_grad + part, (entry_part, expand_part, contract_part), table_term


SPOT = ("section", "core", "zh")
GRID = ("dph", "section")


def spot(section, core, high):
    return 4 * section + 2 * core + high


def routes(layer, far):
    return [
        (spot(layer, block, high), spot(block, high, high ^ far)) for block in range(2) for high in range(2)
    ]


def at_home():
    return lax.axis_index("core") == lax.axis_index("zh")


def spread_weight(shard, layer):
    near, far = (lax.ppermute(shard, SPOT, routes(layer, far)) for far in (0, 1))
    return jnp.where(at_home(), near, far)


def whole_weight(part):
    return lax.all_gather(part, GRID, axis=0, tiled=True)


def reduce_weight(term):
    return lax.psum_scatter(term, GRID, scatter_dimension=0, tiled=True)


def return_weight(part, layer):
    return tuple(lax.ppermute(part, SPOT, [(b, a) for a, b in routes(layer, far)]) for far in (0, 1))


def rows_route(source, target):
    return [(spot(source, core, high), spot(target, high, core)) for core in range(2) for high in range(2)]


def keep_rows(rows):
    return lax.ppermute(rows, SPOT, rows_route(0, 0) + rows_route(1, 1))


def cross_rows(rows):
    return lax.ppermute(rows, SPOT, rows_route(0, 1) + rows_route(1, 0))


def send_rows(rows, layer):
    return lax.ppermute(rows, SPOT, rows_route(layer, layer)), lax.ppermute(rows, SPOT, rows_route(1 - layer, layer))


def sum_everywhere(value, axes):
    for axis in axes:
        step = 1
        while step < lax.axis_size(axis):
            value = value + partner(value, axis, step)
            step *= 2
    return value


def local(
    inputs,
    segment_ids,
    valid_frames,
    segment_codes,
    norm_table,
    entry_weight,
    mixing_weight,
    expand_weight,
    contract_weight,
    cotangent,
):
    section = lax.axis_index("section")
    core, low = lax.axis_index("core"), lax.axis_index("zl")
    low_count = lax.axis_size("zl")
    micro_count, shard_rows, features = inputs.shape
    frames = segment_ids.shape[1]
    code_count = norm_table.shape[1]
    segment_count = segment_codes.shape[1]

    pick = lambda array: lax.dynamic_index_in_dim(array, section, 0, keepdims=False)
    first_section = section == 0
    shards = (
        jnp.concatenate((entry_weight[0].reshape(entry_weight.shape[1], -1), mixing_weight[0].T), axis=1),
        expand_weight[0],
        contract_weight[0].T,
    )
    entry_part = spread_weight(shards[0], 0)
    codes = jnp.pad(pick(segment_codes), (0, frames - segment_count))
    numbers = keep_rows(jnp.stack((pick(segment_ids), pick(valid_frames), codes)))
    segment_row, valid_row, code_row = numbers[0], numbers[1], numbers[2, :segment_count]
    own_input = keep_rows(pick(inputs))
    other_table = partner(norm_table[0], "section")
    tables = (
        jnp.where(first_section, norm_table[0], other_table),
        jnp.where(first_section, other_table, norm_table[0]),
    )
    expand_part = spread_weight(after(shards[1], (own_input, entry_part)), 0)
    contract_part = spread_weight(after(shards[2], (own_input, entry_part)), 0)
    weights = [[whole_weight(part) for part in (entry_part, expand_part, contract_part)]]
    entry_next = spread_weight(after(shards[0], expand_part), 1)
    expand_next = spread_weight(after(shards[1], contract_part), 1)
    contract_next = spread_weight(after(shards[2], entry_next), 1)
    weights.append([whole_weight(part) for part in (entry_next, expand_next, contract_next)])

    rank = core * low_count + low
    ranks = jnp.stack(
        [(core ^ side) * low_count + (low ^ step) for step in range(low_count) for side in range(2)]
    )
    places = (ranks[:, None] * shard_rows + jnp.arange(shard_rows, dtype=jnp.int32)[None, :]).reshape(-1)
    reorder = lambda row: row.reshape(-1, shard_rows)[ranks].reshape(-1)
    segment_rel, valid_rel = reorder(segment_row), reorder(valid_row)
    key_info = jnp.stack((jnp.where(valid_rel == 1, segment_rel, -1), places), axis=1)
    query_info = {
        causal: jnp.stack((segment_rel, places, places if causal else jnp.full_like(places, frames)))
        for causal in (False, True)
    }

    all_places = jnp.arange(frames, dtype=jnp.int32)
    earlier = jnp.concatenate([segment_row[:1] - 1, segment_row[:-1]])
    starts = lax.cummax(jnp.where(segment_row != earlier, all_places, 0), axis=0)
    own_slice = lambda row: lax.dynamic_slice_in_dim(row, rank * shard_rows, shard_rows, 0)
    own_segment = own_slice(segment_row)
    own_offset = own_slice(all_places - starts)
    chosen = (own_segment[:, None] == jnp.arange(segment_count, dtype=jnp.int32)[None, :]).astype(F32)
    code_hot = (code_row[:, None] == jnp.arange(code_count, dtype=jnp.int32)[None, :]).astype(F32)
    context = {"key_info": key_info, "query_info": query_info, "chosen": chosen}

    def frame_table(layer):
        by_segment = jnp.dot(code_hot, tables[layer].reshape(code_count, -1), precision=HIGHEST)
        by_segment = by_segment.reshape(segment_count, 4, features)
        rows = []
        for kind in range(4):
            row = by_segment[0, kind][None, :]
            for segment in range(1, segment_count):
                row = jnp.where(own_segment[:, None] == segment, by_segment[segment, kind][None, :], row)
            rows.append(row)
        return rows

    frame_tables = [frame_table(layer) for layer in range(2)]
    stream = lax.optimization_barrier(own_input.astype(F32) + positions_table(own_offset, features))
    leave = lambda value: value

    other_rows = lax.dynamic_index_in_dim(cotangent[0], 1 - section, 0, keepdims=False)

    def fetch_cotangents(projected):
        return keep_rows(after(pick(cotangent[0]), (projected, contract_next))), cross_rows(
            after(other_rows, (projected, contract_next))
        )

    first, first_saved, (own_cotangent, other_cotangent) = layer_forward(
        stream, context, frame_tables[0], weights[0], True, fetch_cotangents, leave
    )
    cotangents = (
        jnp.where(first_section, own_cotangent, other_cotangent),
        jnp.where(first_section, other_cotangent, own_cotangent),
    )
    first_out = first.astype(BF16)

    def fetch_branch(projected):
        return gather_waves(after(cotangents[1], projected)), send_rows(after(first_out, projected), 0)

    second, second_saved, (branch, first_rows) = layer_forward(
        first_out.astype(F32), context, frame_tables[1], weights[1], False, fetch_branch, leave
    )
    second_out = second.astype(BF16)
    flying = {}

    def send_second(value):
        flying["second"] = send_rows(after(second_out, value), 1)
        return value

    def end(name):
        def hold(value):
            value, flying[name] = together(value, flying[name])
            return value

        return hold

    upper_grad, upper_parts, upper_table = layer_backward(
        second_saved, context, frame_tables[1], weights[1], cotangents[1].astype(F32), branch, False,
        send_second, leave, end("second"),
    )
    upper_round = upper_grad.astype(BF16)
    lower_cotangent = cotangents[0].astype(F32) + upper_grad
    branch = gather_waves(lower_cotangent.astype(BF16))
    flying["upper"] = send_rows(after(upper_round, branch), 1)

    def return_upper(value):
        value = end("upper")(value)
        flying["terms"] = [return_weight(after(part, value), 1) for part in upper_parts[1:]]
        return value

    def return_entry(value):
        flying["terms"].append(return_weight(after(upper_parts[0], value), 1))
        return value

    lower_grad, lower_parts, lower_table = layer_backward(
        first_saved, context, frame_tables[0], weights[0], lower_cotangent, branch, True,
        return_upper, return_entry, end("terms"),
    )
    lower_rows = send_rows(lower_grad.astype(BF16), 0)
    lower_terms = [return_weight(part, 0) for part in (lower_parts[2], lower_parts[1], lower_parts[0])]
    upper_terms = [flying["terms"][1], flying["terms"][0], flying["terms"][2]]
    contract_grad, expand_grad, entry_grad = (
        sum(jnp.where(first_section, lower, upper).astype(F32) for lower, upper in zip(lower_pair, upper_pair))
        for lower_pair, upper_pair in zip(lower_terms, upper_terms)
    )

    def rows_of(lower_pair, upper_pair):
        own, other = (jnp.where(first_section, lower, upper) for lower, upper in zip(lower_pair, upper_pair))
        return jnp.stack((jnp.where(first_section, own, other), jnp.where(first_section, other, own)))[None]

    layer_outputs = rows_of(first_rows, flying["second"])
    input_grads = rows_of(lower_rows, flying["upper"]).astype(F32)

    by_code = lambda term: lax.dot_general(
        code_hot, term.reshape(segment_count, -1), (((0,), (0,)), ((), ())), precision=HIGHEST
    )
    lower_table, upper_table = by_code(lower_table), by_code(upper_table)
    table_grad = jnp.where(first_section, lower_table, upper_table)
    table_grad = table_grad + partner(jnp.where(first_section, upper_table, lower_table), "section")
    table_grad = sum_everywhere(table_grad, ("dph", "core", "zh", "zl")).reshape(norm_table.shape)
    width = entry_grad.shape[1] // 4
    return (
        layer_outputs,
        input_grads,
        entry_grad[:, : 3 * width].reshape(entry_weight.shape),
        entry_grad[:, 3 * width :].T[None],
        expand_grad[None],
        contract_grad.T[None],
        table_grad,
    )


def solution(mesh):
    sections, dp, tensor = (mesh.shape[name] for name in ("section", "dp", "tensor"))
    grid = Mesh(
        mesh.devices.reshape(sections, dp // 2, 2, 2, tensor // 2), ("section", "dph", "core", "zh", "zl")
    )
    row, unit = ("dph", "core"), ("zh", "zl")
    placed = (
        P(row, unit, None),
        P(row, None),
        P(row, None),
        P(row, None),
        P("section", None, None, None),
        P("section", row, None, unit),
        P("section", unit, row),
        P("section", row, unit),
        P("section", unit, row),
        P("section", row, unit, None),
    )
    return jax.shard_map(
        local,
        mesh=grid,
        in_specs=placed,
        out_specs=(
            P("section", row, unit, None),
            P("section", row, unit, None),
            P("section", row, None, unit),
            P("section", unit, row),
            P("section", row, unit),
            P("section", unit, row),
            P("section", None, None, None),
        ),
        check_vma=False,
    )
```

```python
import math

import jax
import jax.numpy as jnp
from jax import lax
from jax.experimental import pallas as pl
from jax.experimental.layout import Layout, with_layout_constraint
from jax.experimental.pallas import tpu as pltpu
from jax.sharding import Mesh, PartitionSpec as P

HEAD_DIM = 64
NORM_EPS = 1e-05
MASKED = -1e30
HIGHEST = lax.Precision.HIGHEST
PAIR = 2 * HEAD_DIM
QUERY_SCALE = 1.0 / math.sqrt(HEAD_DIM)
VMEM_LIMIT = 32 * 2**20
BF16 = jnp.bfloat16
F32 = jnp.float32


def product(left, right, left_dim, right_dim):
    return lax.dot_general(left, right, (((left_dim,), (right_dim,)), ((), ())), preferred_element_type=F32)


def partner(block, axis, step=1):
    return lax.ppermute(block, axis, [(i, i ^ step) for i in range(lax.axis_size(axis))])


def low_parts(piece):
    return [piece] + [partner(piece, "zl", step) for step in range(1, lax.axis_size("zl"))]


def whole_waves(parts):
    return [jnp.concatenate([part, partner(part, "core")], axis=0) for part in parts]


def gather_waves(piece, work):
    waves, results = [], []
    for part in low_parts(piece):
        if results:
            part = after(part, results[-1])
        waves.append(jnp.concatenate([part, partner(part, "core")], axis=0))
        results.append(work(waves[-1]))
    return waves, results


def scatter_waves(term_of):
    total = None
    for step in reversed(range(lax.axis_size("zl"))):
        term = term_of(step)
        half = term.shape[0] // 2
        mine = term[:half] + partner(term[half:].astype(BF16), "core").astype(F32)
        if step:
            mine = partner(mine.astype(BF16), "zl", step).astype(F32)
        total = mine if total is None else total + mine
    return total


def waves_of(array):
    return jnp.split(array, lax.axis_size("zl"), axis=0)


def positions_table(offset, features):
    column = jnp.arange(features, dtype=jnp.int32)
    frequency = jnp.exp(-math.log(10000.0) * (2 * (column // 2)).astype(F32) / features)
    angles = offset.astype(F32)[:, None] * frequency[None, :]
    return jnp.where(column[None, :] % 2 == 0, jnp.sin(angles), jnp.cos(angles))


def normalize(values):
    centred = values - jnp.mean(values, axis=-1, keepdims=True)
    spread = jnp.mean(centred * centred, axis=-1, keepdims=True)
    rate = lax.rsqrt(spread + NORM_EPS)
    return centred * rate, rate


def gelu_pair(x):
    slope = math.sqrt(2.0 / math.pi)
    square = x * x
    bent = jnp.tanh(slope * x * (1.0 + 0.044715 * square))
    half = 0.5 * (1.0 + bent)
    rise = half + 0.5 * x * (1.0 - bent * bent) * (slope * (1.0 + 3.0 * 0.044715 * square))
    return x * half, rise


def head_lanes(block, side):
    lanes = lax.broadcasted_iota(jnp.int32, block.shape, 1)
    return jnp.where(lanes // HEAD_DIM == side, block, jnp.zeros_like(block))


def attend_kernel(
    query_ref, key_ref, value_ref, key_info_ref, query_info_ref, mixed_ref, logsum_ref, bias_ref
):
    key_segment, key_place = key_info_ref[:, 0:1], key_info_ref[:, 1:2]
    query_segment, query_place, last = query_info_ref[0:1, :], query_info_ref[1:2, :], query_info_ref[2:3, :]
    allowed = ((key_segment == query_segment) & (key_place <= last)) | (key_place == query_place)
    bias_ref[...] = jnp.where(allowed, 0.0, MASKED)
    rows, logsums = [], []
    for pair in range(query_ref.shape[1] // PAIR):
        lanes = slice(pair * PAIR, (pair + 1) * PAIR)
        keys, values = key_ref[:, lanes], value_ref[:, lanes]
        queries = query_ref[:, lanes] * QUERY_SCALE
        for side in range(PAIR // HEAD_DIM):
            scores = product(keys, head_lanes(queries, side), 1, 1) + bias_ref[...]
            peak = jnp.max(scores, axis=0, keepdims=True)
            raised = jnp.exp(scores - peak)
            total = jnp.sum(raised, axis=0, keepdims=True)
            mixed = product(values, raised.astype(BF16), 0, 0)
            rows.append(mixed[side * HEAD_DIM : (side + 1) * HEAD_DIM] * (1.0 / total))
            logsums.append(peak + jnp.log(total))
    mixed_ref[...] = jnp.concatenate(rows, axis=0).T.astype(BF16)
    logsum_ref[...] = jnp.concatenate(logsums, axis=0)


def attend(projected, key_info, query_info):
    frames, width = projected.shape[0], projected.shape[1] // 3
    block = min(frames, 256)
    blocks, heads = frames // block, width // HEAD_DIM
    return pl.pallas_call(
        attend_kernel,
        grid=(blocks,),
        in_specs=[
            pl.BlockSpec((block, width), lambda i: (i, 0)),
            pl.BlockSpec((frames, width), lambda i: (0, 1)),
            pl.BlockSpec((frames, width), lambda i: (0, 2)),
            pl.BlockSpec(key_info.shape, lambda i: (0, 0)),
            pl.BlockSpec((query_info.shape[0], block), lambda i: (0, i)),
        ],
        out_specs=[
            pl.BlockSpec((block, width), lambda i: (i, 0)),
            pl.BlockSpec((heads, block), lambda i: (0, i)),
        ],
        out_shape=[
            jax.ShapeDtypeStruct((frames, width), BF16),
            jax.ShapeDtypeStruct((heads, frames), F32),
        ],
        scratch_shapes=[pltpu.VMEM((frames, block), F32)],
        compiler_params=pltpu.CompilerParams(vmem_limit_bytes=VMEM_LIMIT),
        cost_estimate=pl.CostEstimate(
            flops=16 * frames * frames * width,
            bytes_accessed=8 * frames * width,
            transcendentals=heads * frames * frames,
        ),
        name="attend",
    )(projected, projected, projected, key_info, query_info)


def attend_back_kernel(
    query_ref, key_ref, value_ref, key_info_ref, query_info_ref, mixed_ref, logsum_ref, grad_ref, key_sum, value_sum, bias_ref
):
    step = pl.program_id(0)
    block, width = query_ref.shape

    @pl.when(step == 0)
    def _():
        key_sum[...] = jnp.zeros_like(key_sum)
        value_sum[...] = jnp.zeros_like(value_sum)

    key_segment, key_place = key_info_ref[:, 0:1], key_info_ref[:, 1:2]
    query_segment, query_place, last = query_info_ref[0:1, :], query_info_ref[1:2, :], query_info_ref[2:3, :]
    allowed = ((key_segment == query_segment) & (key_place <= last)) | (key_place == query_place)
    bias_ref[...] = jnp.where(allowed, 0.0, MASKED)
    rows = []
    for pair in range(width // PAIR):
        lanes = slice(pair * PAIR, (pair + 1) * PAIR)
        keys, values = key_ref[:, lanes], value_ref[:, lanes]
        queries = query_ref[:, lanes] * QUERY_SCALE
        for side in range(PAIR // HEAD_DIM):
            head = pair * (PAIR // HEAD_DIM) + side
            query_part = head_lanes(queries, side)
            upstream = head_lanes(mixed_ref[:, lanes], side)
            scores = product(keys, query_part, 1, 1) + bias_ref[...]
            probs = jnp.exp(scores - logsum_ref[head : head + 1, :])
            prob_grad = product(values, upstream, 1, 1)
            inner = jnp.sum(probs * prob_grad, axis=0, keepdims=True)
            score_grad = (probs * (prob_grad - inner)).astype(BF16)
            value_sum[:, lanes] += product(probs.astype(BF16), upstream, 1, 0)
            key_sum[:, lanes] += product(score_grad, query_part, 1, 0)
            row = product(keys, score_grad, 0, 0)
            rows.append(row[side * HEAD_DIM : (side + 1) * HEAD_DIM])
    query_grad = jnp.concatenate(rows, axis=0).T * QUERY_SCALE
    grad_ref[pl.ds(pl.multiple_of(step * block, block), block), :width] = query_grad.astype(BF16)

    @pl.when(step == pl.num_programs(0) - 1)
    def _():
        grad_ref[:, width : 2 * width] = key_sum[...].astype(BF16)
        grad_ref[:, 2 * width :] = value_sum[...].astype(BF16)


def attend_back(projected, key_info, query_info, mixture_grad, logsum):
    frames, width = mixture_grad.shape
    block = min(frames, 256)
    blocks, heads = frames // block, width // HEAD_DIM
    return pl.pallas_call(
        attend_back_kernel,
        grid=(blocks,),
        in_specs=[
            pl.BlockSpec((block, width), lambda i: (i, 0)),
            pl.BlockSpec((frames, width), lambda i: (0, 1)),
            pl.BlockSpec((frames, width), lambda i: (0, 2)),
            pl.BlockSpec(key_info.shape, lambda i: (0, 0)),
            pl.BlockSpec((query_info.shape[0], block), lambda i: (0, i)),
            pl.BlockSpec((block, width), lambda i: (i, 0)),
            pl.BlockSpec((heads, block), lambda i: (0, i)),
        ],
        out_specs=pl.BlockSpec((frames, 3 * width), lambda i: (0, 0)),
        out_shape=jax.ShapeDtypeStruct((frames, 3 * width), BF16),
        scratch_shapes=[
            pltpu.VMEM((frames, width), F32),
            pltpu.VMEM((frames, width), F32),
            pltpu.VMEM((frames, block), F32),
        ],
        compiler_params=pltpu.CompilerParams(vmem_limit_bytes=VMEM_LIMIT),
        cost_estimate=pl.CostEstimate(
            flops=40 * frames * frames * width,
            bytes_accessed=14 * frames * width,
            transcendentals=heads * frames * frames,
        ),
        name="attend_back",
    )(projected, projected, projected, key_info, query_info, mixture_grad, logsum)


def after(value, earlier):
    return lax.optimization_barrier((value, earlier))[0]


def together(*values):
    return lax.optimization_barrier(values)


def rows_major(array):
    return with_layout_constraint(array, Layout((0, 1)))


def join(waves):
    return jnp.concatenate(waves, axis=0)


def stretch(sure, body, *args):
    shapes = jax.eval_shape(body, *args)
    blank = lambda *rest: jax.tree.map(lambda leaf: jnp.zeros(leaf.shape, leaf.dtype), shapes)
    return lax.cond(sure, body, blank, *args)


def modulate(values, scale, shift):
    unit, rate = normalize(values)
    return unit, rate, (unit * (1.0 + scale) + shift).astype(BF16)


def first_half(normed, entry, context, causal):
    projected = join([product(wave, entry, 1, 0).astype(BF16) for wave in normed])
    mixture, logsum = attend(projected, context["key_info"], context["query_info"][causal])
    return projected, mixture, logsum


def mix(stream, mixture, mixing):
    waves = waves_of(mixture)
    return stream + scatter_waves(lambda step: product(waves[step], mixing, 1, 1))


def widen(expand):
    def work(wave):
        value, slope = gelu_pair(product(wave, expand, 1, 0))
        return together(value.astype(BF16), slope.astype(BF16))

    return work


def narrow(contract, rise):
    slopes = iter(rise)
    return lambda wave: (product(wave, contract, 1, 0) * next(slopes).astype(F32)).astype(BF16)


def collect(middle, hidden, contract):
    return middle + scatter_waves(lambda step: product(hidden[step], contract, 1, 1))


def norm_back(unit, rate, scale, grad, chosen):
    lifted = grad * (1.0 + scale)
    back = rate * (
        lifted
        - jnp.mean(lifted, axis=-1, keepdims=True)
        - unit * jnp.mean(lifted * unit, axis=-1, keepdims=True)
    )
    scale_sum = lax.dot_general(chosen, grad * unit, (((0,), (0,)), ((), ())), precision=HIGHEST)
    shift_sum = lax.dot_general(chosen, grad, (((0,), (0,)), ((), ())), precision=HIGHEST)
    return back, scale_sum, shift_sum


def wide_terms(gate_grad, branch, expand, second, hidden):
    grad = scatter_waves(lambda step: product(gate_grad[step], expand, 1, 1))
    terms = (product(join(branch), join(hidden), 0, 0), product(join(second), join(gate_grad), 0, 0))
    return grad, rows_major(jnp.concatenate([term.astype(BF16) for term in terms], axis=1))


def back_norm(second_grad, upstream, kept, table, mixing, mixture, context):
    part, scale_sum, shift_sum = norm_back(*kept, table[2], second_grad, context["chosen"])
    middle_grad = upstream + part
    outgoing, mixture_grad = gather_waves(
        middle_grad.astype(BF16), lambda wave: product(wave, mixing, 1, 0).astype(BF16)
    )
    return middle_grad, join(outgoing), join(mixture_grad), (scale_sum, shift_sum)


def back_attention(outgoing, mixture_grad, kept, context, causal):
    normed, projected, mixture, logsum = kept
    projected_grad = attend_back(projected, context["key_info"], context["query_info"][causal], mixture_grad, logsum)
    terms = product(join(normed), projected_grad, 0, 0), product(outgoing, mixture, 0, 0)
    return projected_grad, rows_major(jnp.concatenate([term.astype(BF16) for term in terms], axis=1))


def back_entry(projected_grad, middle_grad, sums, kept, table, entry, context):
    unit_one, rate_one = kept
    waves = waves_of(projected_grad)
    normed_grad = scatter_waves(lambda step: product(waves[step], entry, 1, 1))
    part, scale_sum, shift_sum = norm_back(unit_one, rate_one, table[0], normed_grad, context["chosen"])
    return middle_grad + part, jnp.stack((scale_sum, shift_sum) + sums, axis=1)


SPOT = ("section", "core", "zh")
GRID = ("dph", "section")


def spot(section, core, high):
    return 4 * section + 2 * core + high


def routes(layer, far):
    return [
        (spot(layer, block, high), spot(block, high, high ^ far)) for block in range(2) for high in range(2)
    ]


def hop_weight(shard):
    route = [(spot(1 - block, block, high), spot(block, block, high)) for block in range(2) for high in range(2)]
    other = lax.ppermute(shard, SPOT, route)
    first = lax.axis_index("section") == 0
    return jnp.where(first, shard, other), jnp.where(first, other, shard)


def at_home():
    return lax.axis_index("core") == lax.axis_index("zh")


def spread_weight(shard):
    near, far = (
        lax.ppermute(
            shard, SPOT, [(spot(block, block, high), spot(block, high, high ^ far)) for block in range(2) for high in range(2)]
        )
        for far in (0, 1)
    )
    return jnp.where(at_home(), near, far)


def whole_weight(part):
    return lax.all_gather(part, GRID, axis=0, tiled=True)


def reduce_weight(term):
    return lax.psum_scatter(term, GRID, scatter_dimension=0, tiled=True)


def across(block, step):
    flip = 2 * (step % 2) + step // 2
    return lax.ppermute(block, GRID[::-1], [(i, i ^ flip) for i in range(4)])


def near_blocks(part):
    if lax.axis_size("dph") != 2:
        return (whole_weight(part),)
    return part, across(part, 1), across(part, 2)


def far_block(blocks):
    return (across(blocks[0], 3),) if len(blocks) > 1 else ()


def direct_blocks(part):
    blocks = near_blocks(part)
    return blocks + far_block(blocks)


def direct_sums(term):
    return reduce_near(term) + reduce_far(term)


def assemble(blocks):
    if len(blocks) == 1:
        return blocks[0]
    first = lax.axis_index("section") == 0
    left = lax.axis_index("dph") == 0
    one, two, three, four = blocks
    own = (jnp.where(first, one, two), jnp.where(first, two, one))
    other = (jnp.where(first, three, four), jnp.where(first, four, three))
    order = [jnp.where(left, a, b) for a, b in zip(own + other, other + own)]
    return jnp.concatenate(order, axis=0)


def blocks_of(term, *steps):
    blocks = term.reshape(4, -1, term.shape[1])
    place = 2 * lax.axis_index("dph") + lax.axis_index("section")
    return [lax.dynamic_index_in_dim(blocks, place ^ step, 0, keepdims=False) for step in steps]


def reduce_near(term):
    if lax.axis_size("dph") != 2:
        return (reduce_weight(term),)
    own, one, two = blocks_of(term, 0, 1, 2)
    return own, across(one, 1), across(two, 2)


def reduce_far(term):
    return tuple(across(block, 3) for block in blocks_of(term, 3)) if lax.axis_size("dph") == 2 else ()


def half_sum(term):
    if lax.axis_size("dph") != 2:
        return (reduce_weight(term),)
    parts, place = term.reshape(2, -1, term.shape[1]), lax.axis_index("dph")
    pick = lambda index: lax.dynamic_index_in_dim(parts, index, 0, keepdims=False)
    return pick(place), partner(pick(1 - place), "dph")


def whole_sum(halves):
    if len(halves) == 1:
        return halves[0]
    part = halves[0].astype(F32) + halves[1].astype(F32)
    parts, place = part.reshape(2, -1, part.shape[1]), lax.axis_index("section")
    pick = lambda index: lax.dynamic_index_in_dim(parts, index, 0, keepdims=False)
    return (pick(place) + partner(pick(1 - place).astype(BF16), "section").astype(F32)).astype(BF16)


def total(blocks):
    return sum(block.astype(F32) for block in blocks).astype(BF16)


def return_weight(part, layer):
    return tuple(lax.ppermute(part, SPOT, [(b, a) for a, b in routes(layer, far)]) for far in (0, 1))


def rows_route(source, target):
    return [(spot(source, core, high), spot(target, high, core)) for core in range(2) for high in range(2)]


def keep_rows(rows):
    return lax.ppermute(rows, SPOT, rows_route(0, 0) + rows_route(1, 1))


def cross_rows(rows):
    return lax.ppermute(rows, SPOT, rows_route(0, 1) + rows_route(1, 0))


def send_rows(rows, layer):
    return lax.ppermute(rows, SPOT, rows_route(layer, layer)), lax.ppermute(rows, SPOT, rows_route(1 - layer, layer))


def sum_everywhere(value, axes):
    for axis in axes:
        step = 1
        while step < lax.axis_size(axis):
            value = value + partner(value, axis, step)
            step *= 2
    return value


def local(
    inputs,
    segment_ids,
    valid_frames,
    segment_codes,
    norm_table,
    entry_weight,
    mixing_weight,
    expand_weight,
    contract_weight,
    cotangent,
):
    section = lax.axis_index("section")
    core, low = lax.axis_index("core"), lax.axis_index("zl")
    low_count = lax.axis_size("zl")
    micro_count, shard_rows, features = inputs.shape
    frames = segment_ids.shape[1]
    code_count = norm_table.shape[1]
    segment_count = segment_codes.shape[1]

    pick = lambda array: lax.dynamic_index_in_dim(array, section, 0, keepdims=False)
    first_section = section == 0
    sure = valid_frames[0, 0] >= 0
    units = mixing_weight.shape[1]
    entry_shard = entry_weight[0].reshape(entry_weight.shape[1], -1)
    rest_shard = jnp.concatenate((mixing_weight[0].T, expand_weight[0], contract_weight[0].T), axis=1)
    entry_shard = lax.optimization_barrier(entry_shard)
    entry_hop = hop_weight(entry_shard)
    codes = jnp.pad(pick(segment_codes), (0, frames - segment_count))
    numbers = keep_rows(after(jnp.stack((pick(segment_ids), pick(valid_frames), codes)), entry_shard))
    segment_row, valid_row, code_row = numbers[0], numbers[1], numbers[2, :segment_count]
    own_input = keep_rows(after(pick(inputs), entry_shard))
    other_table = partner(after(norm_table[0], entry_shard), "section")
    tables = (
        jnp.where(first_section, norm_table[0], other_table),
        jnp.where(first_section, other_table, norm_table[0]),
    )
    rest_hop = hop_weight(after(rest_shard, entry_shard))
    entry_part = spread_weight(entry_hop[0])
    other_rows = lax.dynamic_index_in_dim(cotangent[0], 1 - section, 0, keepdims=False)

    rank = core * low_count + low
    ranks = jnp.stack(
        [(core ^ side) * low_count + (low ^ step) for step in range(low_count) for side in range(2)]
    )
    places = (ranks[:, None] * shard_rows + jnp.arange(shard_rows, dtype=jnp.int32)[None, :]).reshape(-1)
    reorder = lambda row: row.reshape(-1, shard_rows)[ranks].reshape(-1)
    segment_rel, valid_rel = reorder(segment_row), reorder(valid_row)
    key_info = jnp.stack((jnp.where(valid_rel == 1, segment_rel, -1), places), axis=1)
    query_info = {
        causal: jnp.stack((segment_rel, places, places if causal else jnp.full_like(places, frames)))
        for causal in (False, True)
    }

    all_places = jnp.arange(frames, dtype=jnp.int32)
    earlier = jnp.concatenate([segment_row[:1] - 1, segment_row[:-1]])
    starts = lax.cummax(jnp.where(segment_row != earlier, all_places, 0), axis=0)
    own_slice = lambda row: lax.dynamic_slice_in_dim(row, rank * shard_rows, shard_rows, 0)
    own_segment = own_slice(segment_row)
    own_offset = own_slice(all_places - starts)
    chosen = (own_segment[:, None] == jnp.arange(segment_count, dtype=jnp.int32)[None, :]).astype(F32)
    code_hot = (code_row[:, None] == jnp.arange(code_count, dtype=jnp.int32)[None, :]).astype(F32)
    context = {"key_info": key_info, "query_info": query_info, "chosen": chosen}

    def frame_table(layer):
        by_segment = jnp.dot(code_hot, tables[layer].reshape(code_count, -1), precision=HIGHEST)
        by_segment = by_segment.reshape(segment_count, 4, features)
        rows = []
        for kind in range(4):
            row = by_segment[0, kind][None, :]
            for segment in range(1, segment_count):
                row = jnp.where(own_segment[:, None] == segment, by_segment[segment, kind][None, :], row)
            rows.append(row)
        return rows

    frame_tables = [frame_table(layer) for layer in range(2)]
    blocks = direct_blocks(entry_part)
    stream = lax.optimization_barrier(own_input.astype(F32) + positions_table(own_offset, features))
    unit_one, rate_one, normed = modulate(stream, frame_tables[0][0], frame_tables[0][1])
    rest_part = spread_weight(after(rest_hop[0], (own_input, entry_part)))
    normed, blocks, rest_part = together(whole_waves(low_parts(normed)), blocks, rest_part)
    entry = assemble(blocks)
    cut = units + expand_weight.shape[2]
    every = jnp.concatenate((entry_hop[1], rest_hop[1]), axis=1)
    moving = direct_blocks(rest_part[:, :cut]), spread_weight(after(every, entry))
    halfway = stretch(sure, lambda *args: first_half(*args, context, True), normed, entry)
    (projected, mixture, logsum), (blocks, every) = together(halfway, moving)
    mixed = assemble(blocks)
    mixing, expand = mixed[:, :units], mixed[:, units:]

    def through(stream, mixture, mixing, expand, table):
        middle = lax.optimization_barrier(mix(stream, mixture, mixing))
        unit, rate, modulated = modulate(middle, table[2], table[3])
        second, pairs = gather_waves(modulated, widen(expand))
        return middle, unit, rate, second, [pair[0] for pair in pairs], [pair[1] for pair in pairs]

    moving = direct_blocks(rest_part[:, cut:])
    passed = stretch(sure, through, stream, mixture, mixing, expand, frame_tables[0])
    (middle, unit_two, rate_two, second, hidden, rise), blocks = together(passed, moving)
    contract = assemble(blocks)
    lower_weights = (entry, mixing, expand, contract)
    lower_kept = (unit_one, rate_one), (unit_two, rate_two), (normed, projected, mixture, logsum), second, hidden, rise

    def turn_layer(middle, hidden, contract, table):
        first_out = collect(middle, hidden, contract).astype(BF16)
        unit, rate, modulated = modulate(first_out.astype(F32), table[0], table[1])
        return first_out, unit, rate, whole_waves(low_parts(modulated))

    moving = direct_blocks(every[:, : 4 * units])
    turned = stretch(sure, turn_layer, middle, hidden, contract, frame_tables[1])
    (first_out, unit_one, rate_one, normed), blocks = together(turned, moving)

    entry = assemble(blocks)
    entry, mixing = entry[:, : 3 * units], entry[:, 3 * units :]
    moving = near_blocks(every[:, 4 * units :]), keep_rows(after(pick(cotangent[0]), entry)), cross_rows(
        after(other_rows, entry)
    )
    halfway = stretch(sure, lambda *args: first_half(*args, context, False), normed, entry)
    (projected, mixture, logsum), (blocks, own, other) = together(halfway, moving)
    cotangents = jnp.where(first_section, own, other), jnp.where(first_section, other, own)

    def settle(stream, mixture, mixing, table):
        middle = lax.optimization_barrier(mix(stream.astype(F32), mixture, mixing))
        unit, rate, modulated = modulate(middle, table[2], table[3])
        return middle, unit, rate, whole_waves(low_parts(modulated))

    moving = far_block(blocks), low_parts(cotangents[1])
    settled = stretch(sure, settle, first_out, mixture, mixing, frame_tables[1])
    (middle, unit_two, rate_two, second), (far, branch) = together(settled, moving)
    wide = assemble(blocks + far)
    expand, contract = wide[:, : wide.shape[1] // 2], wide[:, wide.shape[1] // 2 :]

    def finish(middle, second, expand, contract):
        pairs = [widen(expand)(wave) for wave in second]
        hidden, rise = [pair[0] for pair in pairs], [pair[1] for pair in pairs]
        return collect(middle, hidden, contract).astype(BF16), hidden, rise

    moving = [partner(part, "core") for part in branch]
    finished = stretch(sure, finish, middle, second, expand, contract)
    (second_out, hidden, rise), others = together(finished, moving)
    branch = list(zip(branch, others))
    weights = (entry, mixing, expand, contract)
    kept = (unit_one, rate_one), (unit_two, rate_two), (normed, projected, mixture, logsum), second, hidden, rise

    def start_back(branch, contract, rise, expand, second, hidden):
        branch = [join(wave) if isinstance(wave, tuple) else wave for wave in branch]
        gate_grad = [narrow(contract, rise[step : step + 1])(wave) for step, wave in enumerate(branch)]
        return wide_terms(gate_grad, branch, expand, second, hidden)

    own_of = lambda lower, upper: jnp.where(first_section, lower, upper)
    second_grad, wide_term = stretch(sure, start_back, branch, contract, rise, expand, second, hidden)

    def send_outputs(pin):
        own, other = after((own_of(first_out, second_out), own_of(second_out, first_out)), pin)
        return keep_rows(own), cross_rows(other)


    def back_middle(second_grad, upstream, kept, table, weights, wide_term, causal, beside):
        moving = direct_sums(wide_term)
        stepped = stretch(
            sure, lambda *args: back_norm(*args, context), second_grad, upstream, kept[1], table, weights[1], kept[2][2]
        )
        middle_grad, outgoing, mixture_grad, sums = stepped
        sent = beside(mixture_grad)
        attended = stretch(
            sure, lambda *args: back_attention(*args, context, causal), outgoing, mixture_grad, kept[2]
        )
        (projected_grad, entry_term), moving, sent = together(attended, moving, sent)
        return middle_grad, sums, projected_grad, entry_term, total(moving), sent

    middle_grad, sums, projected_grad, entry_term, wide_part, out_rows = back_middle(
        second_grad, cotangents[1].astype(F32), kept, frame_tables[1], weights, wide_term, False, send_outputs
    )

    def cross_back(projected_grad, middle_grad, sums, kept, table, entry, cotangent):
        upper_grad, table_term = back_entry(projected_grad, middle_grad, sums, kept, table, entry, context)
        upstream = cotangent.astype(F32) + upper_grad
        return upper_grad.astype(BF16), table_term, upstream, whole_waves(low_parts(upstream.astype(BF16)))

    moving = direct_sums(entry_term)
    crossed = stretch(
        sure, cross_back, projected_grad, middle_grad, sums, kept[0], frame_tables[1], weights[0], cotangents[0]
    )
    (upper_grad, upper_table, upstream, branch), parts = together(crossed, moving)

    moving = return_weight(jnp.concatenate((wide_part, total(parts)), axis=1), 1)
    started = stretch(
        sure, start_back, branch, lower_weights[3], lower_kept[5], lower_weights[2], lower_kept[3], lower_kept[4]
    )
    (second_grad, wide_term), upper_terms = together(started, moving)
    middle_grad, sums, projected_grad, entry_term, wide_part, upper_rows = back_middle(
        second_grad, upstream, lower_kept, frame_tables[0], lower_weights, wide_term, True,
        lambda pin: send_rows(after(upper_grad, pin), 1)
    )
    moving = half_sum(entry_term), return_weight(wide_part, 0)
    closed = stretch(
        sure, lambda *args: back_entry(*args, context),
        projected_grad, middle_grad, sums, lower_kept[0], frame_tables[0], lower_weights[0],
    )
    (lower_grad, lower_table), (halves, lower_wide) = together(closed, moving)
    entry_part = whole_sum(halves)
    lower_rows = send_rows(lower_grad.astype(BF16), 0)
    lower_entry = return_weight(entry_part, 0)
    by_code = lambda term: lax.dot_general(
        code_hot, term.reshape(segment_count, -1), (((0,), (0,)), ((), ())), precision=HIGHEST
    )
    lower_table, upper_table = by_code(lower_table), by_code(upper_table)
    table_grad = jnp.where(first_section, lower_table, upper_table)
    table_grad = table_grad + partner(jnp.where(first_section, upper_table, lower_table), "section")
    table_grad = sum_everywhere(table_grad, ("dph", "core", "zh", "zl")).reshape(norm_table.shape)
    wide_width = 2 * expand_weight.shape[2]
    upper_terms = [(array[:, :wide_width], array[:, wide_width:]) for array in upper_terms]
    wide_grad, entry_grad = (
        sum(own_of(lower, upper).astype(F32) for lower, upper in zip(lower_pair, upper_pair))
        for lower_pair, upper_pair in zip((lower_wide, lower_entry), zip(*upper_terms))
    )

    def rows_of(lower_pair, upper_pair):
        own, other = (jnp.where(first_section, lower, upper) for lower, upper in zip(lower_pair, upper_pair))
        return jnp.stack((jnp.where(first_section, own, other), jnp.where(first_section, other, own)))[None]

    own, other = out_rows
    layer_outputs = jnp.stack((own_of(own, other), own_of(other, own)))[None]
    input_grads = rows_of(lower_rows, upper_rows).astype(F32)

    hidden_units = wide_grad.shape[1] // 2
    return (
        layer_outputs,
        input_grads,
        entry_grad[:, : 3 * units].reshape(entry_weight.shape),
        entry_grad[:, 3 * units :].T[None],
        wide_grad[:, hidden_units:][None],
        wide_grad[:, :hidden_units].T[None],
        table_grad,
    )


def solution(mesh):
    sections, dp, tensor = (mesh.shape[name] for name in ("section", "dp", "tensor"))
    grid = Mesh(
        mesh.devices.reshape(sections, dp // 2, 2, 2, tensor // 2), ("section", "dph", "core", "zh", "zl")
    )
    row, unit = ("dph", "core"), ("zh", "zl")
    placed = (
        P(row, unit, None),
        P(row, None),
        P(row, None),
        P(row, None),
        P("section", None, None, None),
        P("section", row, None, unit),
        P("section", unit, row),
        P("section", row, unit),
        P("section", unit, row),
        P("section", row, unit, None),
    )
    return jax.shard_map(
        local,
        mesh=grid,
        in_specs=placed,
        out_specs=(
            P("section", row, unit, None),
            P("section", row, unit, None),
            P("section", row, None, unit),
            P("section", unit, row),
            P("section", row, unit),
            P("section", unit, row),
            P("section", None, None, None),
        ),
        check_vma=False,
    )
```
